32 devices in a mesh: group: 2 (over x), dp: 16 (over z, y, core).
Axes of the slice: x: 2, y: 2, z: 4, core: 2. Of those that a mesh axis runs over, the one named last changes fastest.
Arguments:
- activations: bfloat16 [128, 16, 16, 128], P(('group', 'dp')), parts along dimension 0, may hold values from -6 to 6
- cotangent: bfloat16 [64, 8, 8, 256], P(('group', 'dp')), parts along dimension 0, may hold values from -0.796875 to 0.796875
- shallow_weight: bfloat16 [3456, 128], P('dp'), may hold values from -0.109375 to 0.109375
- shallow_gain: bfloat16 [1, 128], P(None, 'dp'), may hold values from 0.099609375 to 1.8984375
- deep_weight: bfloat16 [3456, 256], P('dp'), may hold values from -0.109375 to 0.109375
- deep_gain: bfloat16 [1, 256], P(None, 'dp'), may hold values from 0.099609375 to 1.8984375
Outputs:
- input_grad: bfloat16 [128, 16, 16, 128], P(('group', 'dp')), parts along dimension 0
- shallow_weight_grad: float32 [6912, 128], P(('group', 'dp')), parts along dimension 0
- shallow_gain_grad: float32 [2, 128], P('group', 'dp'), parts along dimension 0
- deep_weight_grad: float32 [6912, 256], P(('group', 'dp')), parts along dimension 0
- deep_gain_grad: float32 [2, 256], P('group', 'dp'), parts along dimension 0
The draws below stay inside these ranges and needn't reach their ends.
There are 2 independent parts, one for each index of `group`. The reference program is written for one: setup_inputs(seed, part) draws one part's arguments, and reference() takes and returns one part's arrays. A program takes and returns all parts, laid end to end along the dimension named above; an argument that names none is the same for every part. Nothing has to cross between parts.
All inputs are finite; a program needn't handle non-finite values.
Results may differ from the reference program's by a relative error of at most 0.017.
Values may be sent and summed in bfloat16 or wider, within the bound.
A program may use at most 64 MiB of HBM per device.

```python
import jax
import jax.numpy as jnp
from jax import lax

CH1 = 128
CH2 = 256
PD = 4
HW = 16
SAMPLES = 16


def spiked(values, own_key, source, target, blocks, factor):
    def block_of(dim):
        return (jnp.arange(values.shape[dim]) // (values.shape[dim] // blocks)).reshape((-1,) + (1,) * (values.ndim - 1 - dim))

    near = jax.random.permutation(own_key, blocks)[block_of(target)]
    second = (block_of(target) + blocks // 2) % blocks
    return jnp.where((block_of(source) == near) | (block_of(source) == second), factor * values, values)


def levels(rng, shape, shards, low, largest):
    factor_of = 1.0
    for position, shards_of in shards:
        draws = jax.random.uniform(jax.random.fold_in(jax.random.fold_in(rng, 6), position), (shards_of,), jnp.float32, low / len(shards), largest / len(shards))
        factor_of = factor_of * jnp.repeat(jnp.exp(draws), shape[position] // shards_of).reshape((-1,) + (1,) * (len(shape) - 1 - position))
    return factor_of


def gaussian(key, dims, width, most, shards=(), kind=jnp.bfloat16):
    loudness = levels(key, dims, shards, -0.22, 0.18) if shards else 1.0
    entries = jax.random.normal(key, dims, jnp.float32) * width * loudness
    return jnp.minimum(jnp.maximum(entries, -most), most).astype(kind)


def heavy_noise(own_key, shape, deviation, most, cuts, heavy, dtype=jnp.bfloat16):
    values = deviation * jax.random.normal(own_key, shape, jnp.float32)
    if cuts:
        values = values * levels(own_key, shape, cuts, -0.22, 0.18)
    return jnp.clip(spiked(values, jax.random.fold_in(own_key, 3), *heavy), -most, most).astype(dtype)


def setup_inputs(seed: int = 0, part: int = 0) -> dict:
    streams_of = jax.random.split(jax.random.key(seed), 7)
    own_keys = jax.random.split(jax.random.fold_in(streams_of[6], part), 7)
    activations = gaussian(own_keys[0], (SAMPLES * PD, HW, HW, CH1), 1.0, 6.0, ((0, 16),))
    cotangent = heavy_noise(own_keys[1], (SAMPLES * PD // 2, HW // 2, HW // 2, CH2), 0.1, 0.796875, ((0, 16),), (0, 3, 16, 2.0))
    shallow_weight = gaussian(streams_of[2], (27 * CH1, CH1), (27 * CH1) ** -0.5, 0.109375, ((0, 16),))
    shallow_gain = jnp.clip(1.0 + 0.18 * jax.random.normal(streams_of[3], (1, CH1), jnp.float32), 0.099609375, 1.8984375).astype(jnp.bfloat16)
    deep_weight = gaussian(streams_of[4], (27 * CH1, CH2), (27 * CH1) ** -0.5, 0.109375, ((0, 16),))
    deep_gain = jnp.clip(1.0 + 0.18 * jax.random.normal(streams_of[5], (1, CH2), jnp.float32), 0.099609375, 1.8984375).astype(jnp.bfloat16)
    return {"activations": activations, "cotangent": cotangent, "shallow_weight": shallow_weight, "shallow_gain": shallow_gain, "deep_weight": deep_weight, "deep_gain": deep_gain}


def gather_taps(padded, depth_tap, height_tap, cells_shape):
    cells_depth, cells_height, cells_width = cells_shape
    pieces = [padded[depth_tap:depth_tap + cells_depth, height_tap:height_tap + cells_height, width_tap:width_tap + cells_width] for width_tap in range(3)]
    stacked = jnp.concatenate(pieces, axis=3)
    return stacked.reshape(cells_depth * cells_height * cells_width, -1)

def convolve(inputs, weight):
    cells_shape = inputs.shape[:3]
    channels = inputs.shape[3]
    padded = jnp.pad(inputs, ((1, 1), (1, 1), (1, 1), (0, 0)))
    summed = jnp.zeros((cells_shape[0] * cells_shape[1] * cells_shape[2], weight.shape[1]), jnp.float32)
    for depth_tap in range(3):
        for height_tap in range(3):
            stacked = gather_taps(padded, depth_tap, height_tap, cells_shape)
            offset = (depth_tap * 3 + height_tap) * 3 * channels
            summed = summed + jnp.dot(stacked, weight[offset:offset + 3 * channels], preferred_element_type=jnp.float32)
    return summed.reshape(cells_shape[0], cells_shape[1], cells_shape[2], weight.shape[1])

def weight_grad(inputs, grad_out):
    cells_shape = inputs.shape[:3]
    padded = jnp.pad(inputs, ((1, 1), (1, 1), (1, 1), (0, 0)))
    grad_flat = grad_out.reshape(-1, grad_out.shape[3])
    blocks_list = []
    for depth_tap in range(3):
        for height_tap in range(3):
            stacked = gather_taps(padded, depth_tap, height_tap, cells_shape)
            blocks_list.append(lax.dot_general(stacked, grad_flat, (((0,), (0,)), ((), ())), preferred_element_type=jnp.float32))
    return jnp.concatenate(blocks_list, axis=0)

def input_grad_of(grad_out, weight):
    cells_depth, cells_height, cells_width = grad_out.shape[:3]
    channels = weight.shape[0] // 27
    grad_flat = grad_out.reshape(-1, grad_out.shape[3])
    accum = jnp.zeros((cells_depth + 2, cells_height + 2, cells_width + 2, channels), jnp.float32)
    for depth_tap in range(3):
        for height_tap in range(3):
            offset = (depth_tap * 3 + height_tap) * 3 * channels
            product = lax.dot_general(grad_flat, weight[offset:offset + 3 * channels], (((1,), (1,)), ((), ())), preferred_element_type=jnp.float32)
            product = product.reshape(cells_depth, cells_height, cells_width, 3, channels)
            for width_tap in range(3):
                accum = accum.at[depth_tap:depth_tap + cells_depth, height_tap:height_tap + cells_height, width_tap:width_tap + cells_width].add(product[:, :, :, width_tap])
    return accum[1:-1, 1:-1, 1:-1]

def norm_act(hidden, gain_row):
    center = hidden - lax.optimization_barrier(jnp.mean(hidden, axis=(0, 1, 2), keepdims=True))
    spread = lax.optimization_barrier(jnp.mean(center * center, axis=(0, 1, 2), keepdims=True))
    return jax.nn.silu(center * lax.rsqrt(spread + 1e-05) * gain_row[0])

def pool_act(hidden, gain_row):
    active = norm_act(hidden, gain_row)
    cells_depth, cells_height, cells_width, channels = active.shape
    blocks = active.reshape(cells_depth // 2, 2, cells_height // 2, 2, cells_width // 2, 2, channels)
    return lax.optimization_barrier(jnp.mean(blocks, axis=(1, 3, 5)))

def sample_grads(inputs, upstream, shallow_full, shallow_gain, deep_full, deep_gain):
    hidden_one = convolve(inputs, shallow_full)
    pooled_float, back_one = jax.vjp(pool_act, hidden_one, shallow_gain)
    pooled = pooled_float.astype(jnp.bfloat16)
    hidden_two = convolve(pooled, deep_full)
    output_two, back_two = jax.vjp(norm_act, hidden_two, deep_gain)
    grad_hidden_two, grad_deep_gain = back_two(upstream.astype(jnp.float32))
    grad_two = grad_hidden_two.astype(jnp.bfloat16)
    grad_deep = weight_grad(pooled, grad_two)
    grad_pooled = input_grad_of(grad_two, deep_full).astype(jnp.bfloat16)
    grad_hidden_one, grad_shallow_gain = back_one(grad_pooled.astype(jnp.float32))
    grad_one = grad_hidden_one.astype(jnp.bfloat16)
    grad_shallow = weight_grad(inputs, grad_one)
    grad_inputs = input_grad_of(grad_one, shallow_full).astype(jnp.bfloat16)
    return (grad_inputs, grad_shallow, grad_shallow_gain, grad_deep, grad_deep_gain)

def reference(activations, cotangent, shallow_weight, shallow_gain, deep_weight, deep_gain):
    samples_in = activations.reshape(SAMPLES, PD, HW, HW, CH1)
    upstreams = cotangent.reshape(SAMPLES, PD // 2, HW // 2, HW // 2, CH2)
    shallow_float = shallow_gain.astype(jnp.float32)
    deep_float = deep_gain.astype(jnp.float32)

    def advance(carry, pair):
        grad_inputs, grad_shallow, grad_sgain, grad_deep, grad_dgain = sample_grads(pair[0], pair[1], shallow_weight, shallow_float, deep_weight, deep_float)
        carry = (carry[0] + grad_shallow, carry[1] + grad_sgain, carry[2] + grad_deep, carry[3] + grad_dgain)
        return (carry, grad_inputs)
    initial = (jnp.zeros((27 * CH1, CH1), jnp.float32), jnp.zeros((1, CH1), jnp.float32), jnp.zeros((27 * CH1, CH2), jnp.float32), jnp.zeros((1, CH2), jnp.float32))
    totals, grads_in = lax.scan(advance, initial, (samples_in, upstreams))
    return (grads_in.reshape(SAMPLES * PD, HW, HW, CH1), totals[0], totals[1], totals[2], totals[3])
```

```python
import functools

import jax
import jax.numpy as jnp
from jax import lax
from jax.experimental import pallas as pl
from jax.experimental.pallas import tpu as pltpu
from jax.sharding import PartitionSpec as P

MESH = pl.DeviceIdType.MESH
LANES = 128
CONV_DIMS = ("NDHWC", "DHWIO", "NDHWC")
GRAD_DIMS = ("CDHWN", "IDHWO", "DHWNC")


def convolve(inputs, weight):
    kernel = weight.reshape(3, 3, 3, inputs.shape[3], -1)
    return lax.conv_general_dilated(
        inputs[None],
        kernel,
        (1, 1, 1),
        ((1, 1),) * 3,
        dimension_numbers=CONV_DIMS,
        preferred_element_type=jnp.float32,
    )[0]


def weight_grad(inputs, grad_out):
    grad = lax.conv_general_dilated(
        inputs[None],
        grad_out[None],
        (1, 1, 1),
        ((1, 1),) * 3,
        dimension_numbers=GRAD_DIMS,
        preferred_element_type=jnp.float32,
    )
    return grad.reshape(27 * inputs.shape[3], -1)


def transposed(weight):
    channels = weight.shape[0] // 27
    flipped = weight.reshape(27, channels, -1)[::-1]
    return flipped.transpose(0, 2, 1).reshape(-1, channels)


def norm_act(hidden, gain_row):
    center = hidden - jnp.mean(hidden, axis=(0, 1, 2), keepdims=True)
    spread = jnp.mean(center * center, axis=(0, 1, 2), keepdims=True)
    return jax.nn.silu(center * lax.rsqrt(spread + 1e-05) * gain_row[0])


def pool_act(hidden, gain_row):
    active = norm_act(hidden, gain_row)
    cells_depth, cells_height, cells_width, channels = active.shape
    blocks = active.reshape(
        cells_depth // 2, 2, cells_height // 2, 2, cells_width // 2, 2, channels
    )
    return jnp.mean(blocks, axis=(1, 3, 5))


def partners(me, steps):
    bits = [lax.rem(me // 2**step, 2) for step in range(steps)]
    peers = [me + 2**step - 2 ** (step + 1) * bits[step] for step in range(steps)]
    return bits, peers


def greet(peers):
    barrier = pltpu.get_barrier_semaphore()
    for peer in peers:
        pl.semaphore_signal(barrier, inc=1, device_id={"dp": peer}, device_id_type=MESH)
    pl.semaphore_wait(barrier, len(peers))


def gather_kernel(steps, pieces, x_ref, out_ref, send_sem, recv_sem):
    count = 2**steps
    bits, peers = partners(lax.axis_index("dp"), steps)
    starts = [
        sum(bits[low] * (count >> (low + 1)) for low in range(step + 1)) for step in range(steps)
    ]
    for piece in range(pieces):
        out_ref[piece, starts[-1]] = x_ref[piece]
    greet(peers)
    copies = {}
    for wave in range(steps + pieces):
        for piece in range(pieces):
            turn = wave - piece
            if turn >= 1 and turn <= steps:
                copies[piece, turn - 1].wait_recv()
            if turn >= 0 and turn < steps:
                step = steps - 1 - turn
                held = out_ref.at[piece, pl.ds(starts[step], count >> (step + 1))]
                copies[piece, turn] = pltpu.make_async_remote_copy(
                    src_ref=held,
                    dst_ref=held,
                    send_sem=send_sem.at[piece, turn],
                    recv_sem=recv_sem.at[piece, turn],
                    device_id={"dp": peers[step]},
                    device_id_type=MESH,
                )
                copies[piece, turn].start()
    for copy in copies.values():
        copy.wait_send()


def reduce_kernel(steps, pieces, x_ref, out_ref, work_ref, recv_ref, send_sem, recv_sem):
    count = 2**steps
    bits, peers = partners(lax.axis_index("dp"), steps)
    greet(peers)
    copies = {}

    def send(piece, step, source):
        size = count >> (step + 1)
        copies[piece, step] = pltpu.make_async_remote_copy(
            src_ref=source,
            dst_ref=recv_ref.at[piece, pl.ds(size, size)],
            send_sem=send_sem.at[piece, step],
            recv_sem=recv_sem.at[piece, step],
            device_id={"dp": peers[step]},
            device_id_type=MESH,
        )
        copies[piece, step].start()

    def total(piece, step, place):
        size = count >> (step + 1)
        if step == 0:
            mine = x_ref[piece, bits[0] * size + place]
        else:
            mine = work_ref[piece, 2 * size + bits[step] * size + place]
        theirs = recv_ref[piece, size + place]
        return mine.astype(jnp.float32) + theirs.astype(jnp.float32)

    def add_range(piece, step, first, length):
        size = count >> (step + 1)

        def body(index, carry):
            place = first + index
            work_ref[piece, size + place] = total(piece, step, place).astype(jnp.bfloat16)
            return carry

        lax.fori_loop(0, length, body, 0)

    for piece in range(pieces):
        half = count // 2
        send(piece, 0, x_ref.at[piece, pl.ds((1 - bits[0]) * half, half)])
    for wave in range(steps + pieces - 1):
        for piece in range(pieces):
            step = wave - piece
            if step < 0 or step >= steps:
                continue
            copies[piece, step].wait_recv()
            if step == steps - 1:
                out_ref[piece] = total(piece, step, 0)
                continue
            size = count >> (step + 1)
            part = size // 2
            away = (1 - bits[step + 1]) * part
            add_range(piece, step, away, part)
            send(piece, step + 1, work_ref.at[piece, pl.ds(size + away, part)])
            add_range(piece, step, bits[step + 1] * part, part)
    for copy in copies.values():
        copy.wait_send()


def bit_reversed(array, steps):
    split = array.reshape((array.shape[0],) + (2,) * steps + array.shape[2:])
    tail = tuple(range(steps + 1, split.ndim))
    turned = split.transpose((0,) + tuple(range(steps, 0, -1)) + tail)
    return turned.reshape(array.shape)


def gather(packed, count):
    pieces, rows, lanes = packed.shape
    steps = count.bit_length() - 1
    full = pl.pallas_call(
        functools.partial(gather_kernel, steps, pieces),
        out_shape=jax.ShapeDtypeStruct((pieces, count, rows, lanes), packed.dtype),
        in_specs=[pl.BlockSpec(memory_space=pltpu.VMEM)],
        out_specs=pl.BlockSpec(memory_space=pltpu.VMEM),
        scratch_shapes=[pltpu.SemaphoreType.DMA((pieces, steps))] * 2,
        compiler_params=pltpu.CompilerParams(
            collective_id=0, has_side_effects=True, vmem_limit_bytes=24 << 20
        ),
    )(packed)
    return bit_reversed(full, steps)


def reduce_scatter(packed, count):
    pieces, _, rows, lanes = packed.shape
    steps = count.bit_length() - 1
    return pl.pallas_call(
        functools.partial(reduce_kernel, steps, pieces),
        out_shape=jax.ShapeDtypeStruct((pieces, rows, lanes), jnp.float32),
        in_specs=[pl.BlockSpec(memory_space=pltpu.VMEM)],
        out_specs=pl.BlockSpec(memory_space=pltpu.VMEM),
        scratch_shapes=[
            pltpu.VMEM(packed.shape, jnp.bfloat16),
            pltpu.VMEM(packed.shape, jnp.bfloat16),
            pltpu.SemaphoreType.DMA((pieces, steps)),
            pltpu.SemaphoreType.DMA((pieces, steps)),
        ],
        compiler_params=pltpu.CompilerParams(
            collective_id=1, has_side_effects=True, vmem_limit_bytes=40 << 20
        ),
    )(bit_reversed(packed, steps))


def pack(blocks, gains):
    pieces = []
    for block, gain in zip(blocks, gains):
        _, rows, channels = block.shape
        below = -(-(rows + 1) // 16) * 16 - rows
        gain_rows = jnp.pad(
            gain[:, None, :], ((0, 0), (0, below - 1), (0, LANES - gain.shape[1]))
        )
        for lane in range(0, channels, LANES):
            pieces.append(
                jnp.concatenate([block[:, :, lane : lane + LANES], gain_rows], axis=1)
            )
    return jnp.stack(pieces)


def on_device(
    count, activations, cotangent, shallow_weight, shallow_gain, deep_weight, deep_gain
):
    rows, shallow_width = shallow_weight.shape
    deep_width = deep_weight.shape[1]
    shallow_pieces = shallow_width // LANES
    shallow_part, deep_part = shallow_gain.shape[1], deep_gain.shape[1]
    full = gather(
        pack((shallow_weight[None], deep_weight[None]), (shallow_gain, deep_gain))[:, 0], count
    )

    def unpack(first, width):
        lanes = [full[first + index, :, :rows] for index in range(width // LANES)]
        return jnp.concatenate(lanes, axis=2).reshape(count * rows, width)

    shallow_full = unpack(0, shallow_width)
    deep_full = unpack(shallow_pieces, deep_width)
    shallow_gfull = full[0, :, rows, :shallow_part].reshape(1, -1).astype(jnp.float32)
    deep_gfull = full[shallow_pieces, :, rows, :deep_part].reshape(1, -1).astype(jnp.float32)

    hidden_one = convolve(activations, shallow_full)
    pooled_float, back_one = jax.vjp(pool_act, hidden_one, shallow_gfull)
    pooled = pooled_float.astype(jnp.bfloat16)
    hidden_two = convolve(pooled, deep_full)
    _, back_two = jax.vjp(norm_act, hidden_two, deep_gfull)
    grad_hidden_two, grad_dgain = back_two(cotangent.astype(jnp.float32))
    grad_two = grad_hidden_two.astype(jnp.bfloat16)
    grad_deep = weight_grad(pooled, grad_two)
    grad_pooled = convolve(grad_two, transposed(deep_full)).astype(jnp.bfloat16)
    grad_hidden_one, grad_sgain = back_one(grad_pooled.astype(jnp.float32))
    grad_one = grad_hidden_one.astype(jnp.bfloat16)
    grad_shallow = weight_grad(activations, grad_one)
    grad_inputs = convolve(grad_one, transposed(shallow_full)).astype(jnp.bfloat16)

    packed = pack(
        (
            grad_shallow.astype(jnp.bfloat16).reshape(count, rows, -1),
            grad_deep.astype(jnp.bfloat16).reshape(count, rows, -1),
        ),
        (
            grad_sgain.astype(jnp.bfloat16).reshape(count, -1),
            grad_dgain.astype(jnp.bfloat16).reshape(count, -1),
        ),
    )
    shares = reduce_scatter(packed, count)
    shallow_share = jnp.concatenate(
        [shares[index, :rows] for index in range(shallow_pieces)], axis=1
    )
    deep_share = jnp.concatenate(
        [shares[index, :rows] for index in range(shallow_pieces, shares.shape[0])], axis=1
    )
    sgain_share = shares[0, rows : rows + 1, :shallow_part]
    dgain_share = shares[shallow_pieces, rows : rows + 1, :deep_part]
    return (grad_inputs, shallow_share, sgain_share, deep_share, dgain_share)


def solution(mesh):
    in_specs = (
        P(("group", "dp"), None, None, None),
        P(("group", "dp"), None, None, None),
        P("dp", None),
        P(None, "dp"),
        P("dp", None),
        P(None, "dp"),
    )
    out_specs = (
        P(("group", "dp"), None, None, None),
        P(("group", "dp"), None),
        P("group", "dp"),
        P(("group", "dp"), None),
        P("group", "dp"),
    )
    return jax.shard_map(
        functools.partial(on_device, mesh.shape["dp"]),
        mesh=mesh,
        in_specs=in_specs,
        out_specs=out_specs,
        check_vma=False,
    )
```

```python
import functools

import jax
import jax.numpy as jnp
from jax import lax
from jax.experimental import pallas as pl
from jax.experimental.pallas import tpu as pltpu
from jax.sharding import PartitionSpec as P

MESH = pl.DeviceIdType.MESH
LANES = 128
CONV_DIMS = ("NDHWC", "DHWIO", "NDHWC")
GRAD_DIMS = ("CDHWN", "IDHWO", "DHWNC")


def convolve(inputs, weight):
    kernel = weight.reshape(3, 3, 3, inputs.shape[3], -1)
    return lax.conv_general_dilated(
        inputs[None],
        kernel,
        (1, 1, 1),
        ((1, 1),) * 3,
        dimension_numbers=CONV_DIMS,
        preferred_element_type=jnp.float32,
    )[0]


def weight_grad(inputs, grad_out):
    grad = lax.conv_general_dilated(
        inputs[None],
        grad_out[None],
        (1, 1, 1),
        ((1, 1),) * 3,
        dimension_numbers=GRAD_DIMS,
        preferred_element_type=jnp.float32,
    )
    return grad.reshape(27 * inputs.shape[3], -1)


def transposed(weight):
    channels = weight.shape[0] // 27
    flipped = weight.reshape(27, channels, -1)[::-1]
    return flipped.transpose(0, 2, 1).reshape(-1, channels)


def norm_act(hidden, gain_row):
    center = hidden - jnp.mean(hidden, axis=(0, 1, 2), keepdims=True)
    spread = jnp.mean(center * center, axis=(0, 1, 2), keepdims=True)
    return jax.nn.silu(center * lax.rsqrt(spread + 1e-05) * gain_row[0])


def pool_act(hidden, gain_row):
    active = norm_act(hidden, gain_row)
    cells_depth, cells_height, cells_width, channels = active.shape
    blocks = active.reshape(
        cells_depth // 2, 2, cells_height // 2, 2, cells_width // 2, 2, channels
    )
    return jnp.mean(blocks, axis=(1, 3, 5))


def partners(me, steps):
    bits = [lax.rem(me // 2**step, 2) for step in range(steps)]
    peers = [me + 2**step - 2 ** (step + 1) * bits[step] for step in range(steps)]
    return bits, peers


def greet(peers):
    barrier = pltpu.get_barrier_semaphore()
    for peer in peers:
        pl.semaphore_signal(barrier, inc=1, device_id={"dp": peer}, device_id_type=MESH)
    pl.semaphore_wait(barrier, len(peers))


def lowest(mask):
    return (mask & -mask).bit_length() - 1


def chunk_of(bits, mask):
    return sum(
        ((1 - bit) if mask >> step & 1 else bit) * 2**step for step, bit in enumerate(bits)
    )


def send_order(steps):
    masks = [mask for mask in range(1, 2**steps) if lowest(mask) > 0]

    def key(mask):
        step = lowest(mask)
        return 1 - (mask - 2**step) / 2**steps + 0.3 * (step - 1)

    return sorted(masks, key=key)


def gather_kernel(steps, pieces, x_ref, out_ref, send_sem, recv_sem):
    bits, peers = partners(lax.axis_index("dp"), steps)
    mine = chunk_of(bits, 0)
    for piece in range(pieces):
        out_ref[piece, mine] = x_ref[piece]
    greet(peers)
    sends = []

    def copy_of(piece, mask, step):
        held = out_ref.at[piece, chunk_of(bits, mask)]
        there = mask | 1 << step
        return pltpu.make_async_remote_copy(
            src_ref=held,
            dst_ref=held,
            send_sem=send_sem.at[piece, there],
            recv_sem=recv_sem.at[piece, there],
            device_id={"dp": peers[step]},
            device_id_type=MESH,
        )

    def send(piece, mask, step):
        copy = copy_of(piece, mask, step)
        copy.start()
        sends.append(copy)

    def arrive(piece, mask):
        landed = out_ref.at[piece, chunk_of(bits, mask)]
        pltpu.make_async_remote_copy(
            src_ref=landed,
            dst_ref=landed,
            send_sem=send_sem.at[piece, mask],
            recv_sem=recv_sem.at[piece, mask],
            device_id={"dp": peers[lowest(mask)]},
            device_id_type=MESH,
        ).wait_recv()

    for step in reversed(range(steps)):
        for piece in range(pieces):
            send(piece, 0, step)
    for mask in reversed(send_order(steps)):
        for piece in range(pieces):
            arrive(piece, mask)
            for step in reversed(range(lowest(mask))):
                send(piece, mask, step)
    for piece in range(pieces):
        for mask in range(1, 2**steps, 2):
            arrive(piece, mask)
    for copy in sends:
        copy.wait_send()


def reduce_kernel(steps, pieces, x_ref, out_ref, work_ref, recv_ref, send_sem, recv_sem):
    bits, peers = partners(lax.axis_index("dp"), steps)
    greet(peers)
    copies = {}

    def send(piece, mask, source):
        copies[piece, mask] = pltpu.make_async_remote_copy(
            src_ref=source,
            dst_ref=recv_ref.at[piece, mask],
            send_sem=send_sem.at[piece, mask],
            recv_sem=recv_sem.at[piece, mask],
            device_id={"dp": peers[lowest(mask)]},
            device_id_type=MESH,
        )
        copies[piece, mask].start()

    def total(piece, mask, count):
        value = x_ref[piece, chunk_of(bits, mask)].astype(jnp.float32)
        for step in range(count):
            copies[piece, mask | 1 << step].wait_recv()
            value = value + recv_ref[piece, mask | 1 << step].astype(jnp.float32)
        return value

    for mask in reversed(range(1, 2**steps, 2)):
        for piece in range(pieces):
            send(piece, mask, x_ref.at[piece, chunk_of(bits, mask)])
    for mask in send_order(steps):
        for piece in range(pieces):
            work_ref[piece, mask] = total(piece, mask, lowest(mask)).astype(jnp.bfloat16)
            send(piece, mask, work_ref.at[piece, mask])
    for piece in range(pieces):
        out_ref[piece] = total(piece, 0, steps)
    for copy in copies.values():
        copy.wait_send()


def gather(packed, count):
    pieces, rows, lanes = packed.shape
    steps = count.bit_length() - 1
    return pl.pallas_call(
        functools.partial(gather_kernel, steps, pieces),
        out_shape=jax.ShapeDtypeStruct((pieces, count, rows, lanes), packed.dtype),
        in_specs=[pl.BlockSpec(memory_space=pltpu.VMEM)],
        out_specs=pl.BlockSpec(memory_space=pltpu.VMEM),
        scratch_shapes=[pltpu.SemaphoreType.DMA((pieces, count))] * 2,
        compiler_params=pltpu.CompilerParams(
            collective_id=0, has_side_effects=True, vmem_limit_bytes=24 << 20
        ),
    )(packed)


def reduce_scatter(packed, count):
    pieces, _, rows, lanes = packed.shape
    steps = count.bit_length() - 1
    return pl.pallas_call(
        functools.partial(reduce_kernel, steps, pieces),
        out_shape=jax.ShapeDtypeStruct((pieces, rows, lanes), jnp.float32),
        in_specs=[pl.BlockSpec(memory_space=pltpu.VMEM)],
        out_specs=pl.BlockSpec(memory_space=pltpu.VMEM),
        scratch_shapes=[
            pltpu.VMEM(packed.shape, jnp.bfloat16),
            pltpu.VMEM(packed.shape, jnp.bfloat16),
            pltpu.SemaphoreType.DMA((pieces, count)),
            pltpu.SemaphoreType.DMA((pieces, count)),
        ],
        compiler_params=pltpu.CompilerParams(
            collective_id=1, has_side_effects=True, vmem_limit_bytes=40 << 20
        ),
    )(packed)


def pack(blocks, gains):
    pieces = []
    for block, gain in zip(blocks, gains):
        _, rows, channels = block.shape
        below = -(-(rows + 1) // 16) * 16 - rows
        gain_rows = jnp.pad(
            gain[:, None, :], ((0, 0), (0, below - 1), (0, LANES - gain.shape[1]))
        )
        for lane in range(0, channels, LANES):
            pieces.append(
                jnp.concatenate([block[:, :, lane : lane + LANES], gain_rows], axis=1)
            )
    return jnp.stack(pieces)


def on_device(
    count, activations, cotangent, shallow_weight, shallow_gain, deep_weight, deep_gain
):
    rows, shallow_width = shallow_weight.shape
    deep_width = deep_weight.shape[1]
    shallow_pieces = shallow_width // LANES
    shallow_part, deep_part = shallow_gain.shape[1], deep_gain.shape[1]
    full = gather(
        pack((shallow_weight[None], deep_weight[None]), (shallow_gain, deep_gain))[:, 0], count
    )

    def unpack(first, width):
        lanes = [full[first + index, :, :rows] for index in range(width // LANES)]
        return jnp.concatenate(lanes, axis=2).reshape(count * rows, width)

    shallow_full = unpack(0, shallow_width)
    deep_full = unpack(shallow_pieces, deep_width)
    shallow_gfull = full[0, :, rows, :shallow_part].reshape(1, -1).astype(jnp.float32)
    deep_gfull = full[shallow_pieces, :, rows, :deep_part].reshape(1, -1).astype(jnp.float32)

    hidden_one = convolve(activations, shallow_full)
    pooled_float, back_one = jax.vjp(pool_act, hidden_one, shallow_gfull)
    pooled = pooled_float.astype(jnp.bfloat16)
    hidden_two = convolve(pooled, deep_full)
    _, back_two = jax.vjp(norm_act, hidden_two, deep_gfull)
    grad_hidden_two, grad_dgain = back_two(cotangent.astype(jnp.float32))
    grad_two = grad_hidden_two.astype(jnp.bfloat16)
    grad_deep = weight_grad(pooled, grad_two)
    grad_pooled = convolve(grad_two, transposed(deep_full)).astype(jnp.bfloat16)
    grad_hidden_one, grad_sgain = back_one(grad_pooled.astype(jnp.float32))
    grad_one = grad_hidden_one.astype(jnp.bfloat16)
    grad_shallow = weight_grad(activations, grad_one)
    grad_inputs = convolve(grad_one, transposed(shallow_full)).astype(jnp.bfloat16)

    packed = pack(
        (
            grad_shallow.astype(jnp.bfloat16).reshape(count, rows, -1),
            grad_deep.astype(jnp.bfloat16).reshape(count, rows, -1),
        ),
        (
            grad_sgain.astype(jnp.bfloat16).reshape(count, -1),
            grad_dgain.astype(jnp.bfloat16).reshape(count, -1),
        ),
    )
    shares = reduce_scatter(packed, count)
    shallow_share = jnp.concatenate(
        [shares[index, :rows] for index in range(shallow_pieces)], axis=1
    )
    deep_share = jnp.concatenate(
        [shares[index, :rows] for index in range(shallow_pieces, shares.shape[0])], axis=1
    )
    sgain_share = shares[0, rows : rows + 1, :shallow_part]
    dgain_share = shares[shallow_pieces, rows : rows + 1, :deep_part]
    return (grad_inputs, shallow_share, sgain_share, deep_share, dgain_share)


def solution(mesh):
    in_specs = (
        P(("group", "dp"), None, None, None),
        P(("group", "dp"), None, None, None),
        P("dp", None),
        P(None, "dp"),
        P("dp", None),
        P(None, "dp"),
    )
    out_specs = (
        P(("group", "dp"), None, None, None),
        P(("group", "dp"), None),
        P("group", "dp"),
        P(("group", "dp"), None),
        P("group", "dp"),
    )
    return jax.shard_map(
        functools.partial(on_device, mesh.shape["dp"]),
        mesh=mesh,
        in_specs=in_specs,
        out_specs=out_specs,
        check_vma=False,
    )
```
